128 devices in a mesh: grp: 4 (over z_hi, core), dev: 32 (over z_lo, x, y).
Axes of the slice: x: 4, y: 4, z: 4 (z_hi: 2, z_lo: 2; z = z_hi * 2 + z_lo), core: 2. Of those that a mesh axis runs over, the one named last changes fastest.
Arguments:
- images: bfloat16 [131072, 1152], P(('grp', 'dev')), may hold values from -60 to 60
- texts: bfloat16 [131072, 1152], P(('grp', 'dev')), may hold values from -60 to 60
- log_scale: float32 [1], replicated, may hold values from 1.6 to 2.6
- logit_bias: float32 [1], replicated, may hold values from -4 to -1
Outputs:
- grad_images: float32 [131072, 1152], P(('grp', 'dev'))
- grad_texts: float32 [131072, 1152], P(('grp', 'dev'))
The draws below stay inside these ranges and needn't reach their ends.
All inputs are finite; a program needn't handle non-finite values.
Results may differ from the reference program's by a relative error of at most 0.004.
Values may be sent and summed in bfloat16 or wider, within the bound.
No kernel may reach another device: no remote copies, remote signals or barrier semaphores. Data moves between devices by JAX's collectives and lax.ppermute only.
A program may use at most 128 MiB of HBM per device.

```python
import jax
import jax.numpy as jnp
from jax import lax

D = 1152
ROWS_DEV = 1024
ROWS = 131072


def scaled_rows(key, base, row_low, row_high, col_low, col_high):
    key_rows, key_cols = jax.random.split(key)
    row_scale = jnp.exp(jax.random.uniform(key_rows, (ROWS, 1), jnp.float32, jnp.log(row_low), jnp.log(row_high)))
    col_scale = jnp.exp(jax.random.uniform(key_cols, (1, D), jnp.float32, jnp.log(col_low), jnp.log(col_high)))
    return base * row_scale * col_scale


def draw_images(key, part):
    key = jax.random.fold_in(key, 11)
    key_base = jax.random.fold_in(key, 0)
    key_scale = jax.random.fold_in(key, 2)
    base = jnp.clip(jax.random.normal(key_base, (ROWS, D), jnp.float32), -6.0, 6.0)
    values = scaled_rows(key_scale, base, 0.3, 3.0, 0.3, 3.0)
    return values.astype(jnp.bfloat16)


def draw_texts(key, part):
    key = jax.random.fold_in(key, 23)
    key_base = jax.random.fold_in(key, 0)
    key_scale = jax.random.fold_in(key, 2)
    base = jnp.clip(jax.random.normal(key_base, (ROWS, D), jnp.float32), -6.0, 6.0)
    values = scaled_rows(key_scale, base, 0.3, 3.0, 0.3, 3.0)
    return values.astype(jnp.bfloat16)


def setup_inputs(seed: int = 0) -> dict:
    keys = jax.random.split(jax.random.key(seed), 5)
    images = draw_images(jax.random.fold_in(keys[4], 71), 0)
    texts = draw_texts(jax.random.fold_in(keys[4], 71), 0)
    log_scale = jnp.clip(jax.random.uniform(keys[2], (1,), jnp.float32, 1.6, 2.6), 1.6, 2.6)
    logit_bias = jnp.clip(jax.random.uniform(keys[3], (1,), jnp.float32, -4.0, -1.0), -4.0, -1.0)
    return {"images": images, "texts": texts, "log_scale": log_scale, "logit_bias": logit_bias}


epsilon = 1e-06

def normalize(raw_rows):
    rows32 = raw_rows.astype(jnp.float32)
    inverse = lax.rsqrt(lax.optimization_barrier(jnp.sum(rows32 * rows32, axis=1, keepdims=True)) + epsilon)
    return (rows32 * inverse, inverse)

def pair_block(picture, caption, temper, offset, diagonal):
    logits = temper * lax.dot_general(picture, caption, (((1,), (1,)), ((), ())), preferred_element_type=jnp.float32) + offset
    weights = jax.nn.sigmoid(logits)
    if diagonal:
        across = lax.broadcasted_iota(jnp.int32, logits.shape, 0)
        down = lax.broadcasted_iota(jnp.int32, logits.shape, 1)
        weights = weights - jnp.where(across == down, 1.0, 0.0).astype(weights.dtype)
    weights_b = weights.astype(jnp.bfloat16)
    toward_img = jnp.dot(weights_b, caption, preferred_element_type=jnp.float32)
    toward_txt = lax.dot_general(weights_b, picture, (((0,), (0,)), ((), ())), preferred_element_type=jnp.float32)
    return (toward_img, toward_txt)

def project_back(unit_rows, grad_unit, inverse):
    along = lax.optimization_barrier(jnp.sum(unit_rows * grad_unit, axis=1, keepdims=True))
    return (grad_unit - unit_rows * along) * inverse

def reference(images, texts, log_scale, logit_bias):
    temper = jnp.exp(log_scale[0])
    offset = logit_bias[0]
    unit_img, inv_img = normalize(images)
    unit_txt, inv_txt = normalize(texts)
    blocks = ROWS // ROWS_DEV
    img_blocks = unit_img.astype(jnp.bfloat16).reshape(blocks, ROWS_DEV, D)
    txt_blocks = unit_txt.astype(jnp.bfloat16).reshape(blocks, ROWS_DEV, D)

    def one_block(block_index, carry):
        grad_x, grad_y = carry
        picture = img_blocks[block_index]
        sum_img = jnp.zeros((ROWS_DEV, D), jnp.float32)
        for back_step in range(3):
            target = ((block_index - back_step) % blocks).astype(jnp.int32)
            toward_img, toward_txt = pair_block(picture, txt_blocks[target], temper, offset, back_step == 0)
            sum_img = sum_img + toward_img
            grad_y = grad_y.at[target].add(toward_txt)
        grad_x = grad_x.at[block_index].set(temper * sum_img)
        return (grad_x, grad_y)
    start = (jnp.zeros((blocks, ROWS_DEV, D), jnp.float32), jnp.zeros((blocks, ROWS_DEV, D), jnp.float32))
    grad_x, grad_y = lax.fori_loop(0, blocks, one_block, start)
    grad_x = grad_x.reshape(ROWS, D)
    grad_y = temper * grad_y.reshape(ROWS, D)
    return (project_back(unit_img, grad_x, inv_img), project_back(unit_txt, grad_y, inv_txt))
```

```python
import functools

import jax
import jax.numpy as jnp
from jax import lax
from jax.experimental import pallas as pl
from jax.experimental.pallas import tpu as pltpu
from jax.sharding import PartitionSpec as P

epsilon = 1e-06
axes = ("grp", "dev")
cuts = (0, 768, 1024)
tile = 256


def passed_along(value, steps):
    count = lax.axis_size(axes)
    pairs = [(source, (source + steps) % count) for source in range(count)]
    return lax.ppermute(value, axes, pairs)


def normalize(raw_rows):
    rows32 = raw_rows.astype(jnp.float32)
    inverse = lax.rsqrt(jnp.sum(rows32 * rows32, axis=1, keepdims=True) + epsilon)
    return rows32 * inverse, inverse


def project_back(unit_rows, grad_unit, inverse):
    along = jnp.sum(unit_rows * grad_unit, axis=1, keepdims=True)
    return (grad_unit - unit_rows * along) * inverse


def attend(own, others, temper, offset, first_row):
    logits = (
        temper
        * lax.dot_general(own, others, (((1,), (1,)), ((), ())), preferred_element_type=jnp.float32)
        + offset
    )
    weights = jax.nn.sigmoid(logits)
    if first_row is not None:
        across = lax.broadcasted_iota(jnp.int32, logits.shape, 0) + first_row
        down = lax.broadcasted_iota(jnp.int32, logits.shape, 1)
        weights = weights - jnp.where(across == down, 1.0, 0.0)
    return jnp.dot(weights.astype(jnp.bfloat16), others, preferred_element_type=jnp.float32)


def kernel(pieces, diagonal, last, temper_ref, offset_ref, *refs):
    img_ref, txt_ref = refs[:2]
    txt_pieces, img_pieces = refs[2 : 2 + pieces], refs[2 + pieces : 2 + 2 * pieces]
    rest = refs[2 + 2 * pieces :]
    if not diagonal:
        (gx_ref, gy_ref), rest = rest[:2], rest[2:]
    out_x, out_y, txt_unit, img_unit = rest
    step = pl.program_id(0)
    temper, offset = temper_ref[0], offset_ref[0]

    @pl.when(step == 0)
    def _():
        for piece_refs, unit_ref in ((txt_pieces, txt_unit), (img_pieces, img_unit)):
            at = 0
            for piece in piece_refs:
                for start in range(0, piece.shape[0], 128):
                    unit, _ = normalize(piece[start : start + 128])
                    unit_ref[at : at + 128] = unit.astype(jnp.bfloat16)
                    at += 128

    first_row = step * tile if diagonal else None
    sides = ((img_ref, txt_unit, out_x), (txt_ref, img_unit, out_y))
    for side, (own_ref, others, out) in enumerate(sides):
        unit, inverse = normalize(own_ref[...])
        total = attend(unit.astype(jnp.bfloat16), others[...], temper, offset, first_row)
        if not diagonal:
            total = total + (gx_ref, gy_ref)[side][...]
        if last:
            total = project_back(unit, temper * total, inverse)
        out[...] = total


def block_sums(temper, offset, images, texts, txt_pieces, img_pieces, sums, last):
    rows, width = images.shape
    pieces = len(txt_pieces)
    others = sum(piece.shape[0] for piece in txt_pieces)
    scalar = pl.BlockSpec(memory_space=pltpu.SMEM)
    rows_spec = pl.BlockSpec((tile, width), lambda i: (i, 0))
    whole = [pl.BlockSpec(piece.shape, lambda i: (0, 0)) for piece in txt_pieces]
    diagonal = not sums
    return pl.pallas_call(
        functools.partial(kernel, pieces, diagonal, last),
        grid=(rows // tile,),
        in_specs=[scalar, scalar, rows_spec, rows_spec] + whole * 2 + [rows_spec] * len(sums),
        out_specs=[rows_spec] * 2,
        out_shape=[jax.ShapeDtypeStruct((rows, width), jnp.float32)] * 2,
        scratch_shapes=[pltpu.VMEM((others, width), jnp.bfloat16)] * 2,
        compiler_params=pltpu.CompilerParams(vmem_limit_bytes=40 * 2**20),
        cost_estimate=pl.CostEstimate(
            flops=8 * rows * others * width, bytes_accessed=16 * rows * width, transcendentals=0
        ),
    )(temper, offset, images, texts, *txt_pieces, *img_pieces, *sums)


def local(images, texts, log_scale, logit_bias):
    temper = jnp.exp(log_scale)
    near_txt, near_img, far_txt, far_img = [], [], [], []
    for low, high in zip(cuts, cuts[1:]):
        near_txt.append(passed_along(texts[low:high], 1))
        near_img.append(passed_along(images[low:high], -1))
    for txt, img in zip(near_txt, near_img):
        far_txt.append(passed_along(txt, 1))
        far_img.append(passed_along(img, -1))
    blocks = functools.partial(block_sums, temper, logit_bias, images, texts)
    sums = blocks([texts], [images], (), False)
    sums = blocks(near_txt, near_img, sums, False)
    sums = blocks(far_txt[:1], far_img[:1], sums, False)
    return tuple(blocks(far_txt[1:], far_img[1:], sums, True))


def solution(mesh):
    return jax.shard_map(
        local,
        mesh=mesh,
        in_specs=(P(axes, None), P(axes, None), P(), P()),
        out_specs=(P(axes, None), P(axes, None)),
        check_vma=False,
    )
```

```python
import functools

import jax
import jax.numpy as jnp
from jax import lax
from jax.experimental import pallas as pl
from jax.experimental.pallas import tpu as pltpu
from jax.sharding import PartitionSpec as P


epsilon = 1e-06
axes = ("grp", "dev")
split = 768
tile = 256
lanes = 128


def exchanged(value, inner):
    count = lax.axis_size(axes)
    first = 0 if inner else 1
    pairs = []
    for low in range(first, count, 2):
        high = (low + 1) % count
        pairs += [(low, high), (high, low)]
    return lax.ppermute(value, axes, pairs)


def on_even(is_even, is_odd):
    odd = lax.rem(lax.axis_index("dev"), 2)
    pl.when(odd == 0)(is_even)
    pl.when(odd == 1)(is_odd)


def normalize(raw_rows):
    rows32 = raw_rows.astype(jnp.float32)
    inverse = lax.rsqrt(jnp.sum(rows32 * rows32, axis=1, keepdims=True) + epsilon)
    return rows32 * inverse, inverse


def unit_rows(pieces, unit_ref):
    base = 0
    for piece in pieces:
        for start in range(0, piece.shape[0], 128):
            unit, _ = normalize(piece[start : start + 128, :])
            unit_ref[base : base + 128, :] = unit.astype(jnp.bfloat16)
            base += 128


def attend(own, others, temper, offset, first_row=None):
    logits = (
        temper
        * lax.dot_general(own, others, (((1,), (1,)), ((), ())), preferred_element_type=jnp.float32)
        + offset
    )
    weights = jax.nn.sigmoid(logits)
    if first_row is not None:
        across = lax.broadcasted_iota(jnp.int32, logits.shape, 0) + first_row
        down = lax.broadcasted_iota(jnp.int32, logits.shape, 1)
        weights = weights - jnp.where(across == down, 1.0, 0.0)
    return jnp.dot(weights.astype(jnp.bfloat16), others, preferred_element_type=jnp.float32)


def piece_kernel(inner, first, img_ref, txt_ref, *refs):
    *_, out_ref, sem = refs

    def fetch(raw_ref):
        copy = pltpu.make_async_copy(raw_ref.at[pl.ds(first, out_ref.shape[0]), :], out_ref, sem)
        copy.start()
        copy.wait()

    inner_ref, outer_ref = functools.partial(fetch, txt_ref), functools.partial(fetch, img_ref)
    on_even(inner_ref, outer_ref) if inner else on_even(outer_ref, inner_ref)


def gate_kernel(*refs):
    del refs


def own_kernel(temper_ref, offset_ref, img_ref, txt_ref, *outs):
    raws, sums, units, inverses = outs[:2], outs[2:4], outs[4:6], outs[6:]
    temper, offset = temper_ref[0], offset_ref[0]

    def take(*sources):
        for source, raw in zip(sources, raws):
            raw[...] = source[...]

    on_even(lambda: take(txt_ref, img_ref), lambda: take(img_ref, txt_ref))
    for raw, unit_ref, inverse_ref in zip(raws, units, inverses):

        @pl.loop(0, raw.shape[0] // 128)
        def _(i, raw=raw, unit_ref=unit_ref, inverse_ref=inverse_ref):
            rows = pl.ds(pl.multiple_of(i * 128, 128), 128)
            unit, inverse = normalize(raw[rows, :])
            unit_ref[rows, :] = unit.astype(jnp.bfloat16)
            inverse_ref[rows, :] = jnp.broadcast_to(inverse, (128, lanes))

    @pl.loop(0, img_ref.shape[0] // tile)
    def _(i):
        first = pl.multiple_of(i * tile, tile)
        rows = pl.ds(first, tile)
        for side in range(2):
            sums[side][rows, :] = attend(
                units[side][rows, :], units[1 - side][...], temper, offset, first
            )


def more_kernel(pieces, onward, temper_ref, offset_ref, own_unit, sum_ref, *refs):
    piece_refs, (out_ref, *onward_refs, others) = refs[:pieces], refs[pieces:]
    temper, offset = temper_ref[0], offset_ref[0]
    unit_rows(piece_refs, others)
    if onward:
        onward_refs[0][...] = piece_refs[-1][...]
    for first in range(0, own_unit.shape[0], tile):
        rows = pl.ds(first, tile)
        out_ref[rows, :] = sum_ref[rows, :] + attend(
            own_unit[rows, :], others[...], temper, offset
        )


def last_kernel(inner, temper_ref, offset_ref, own_unit, sum_ref, raw_ref, inverse_ref, *refs):
    piece, *refs = refs if inner else (refs[0], *refs[3:])
    grad_img, grad_txt, others, ready, sems = refs
    temper, offset = temper_ref[0], offset_ref[0]
    unit_rows([piece], others)

    def copies(into, first):
        rows = pl.ds(first, tile)
        return pltpu.make_async_copy(ready.at[rows, :], into.at[rows, :], sems.at[first // tile])

    def on_target(do):
        into_txt, into_img = functools.partial(do, grad_txt), functools.partial(do, grad_img)
        on_even(into_txt, into_img) if inner else on_even(into_img, into_txt)

    for first in range(0, own_unit.shape[0], tile):
        rows = pl.ds(first, tile)
        total = sum_ref[rows, :] + attend(own_unit[rows, :], others[...], temper, offset)
        raw = raw_ref[rows, :].astype(jnp.float32)
        inverse = inverse_ref[rows, :1]
        scale = temper * inverse
        along = jnp.sum(raw * total, axis=1, keepdims=True)
        ready[rows, :] = scale * total - (scale * inverse * inverse * along) * raw
        on_target(lambda into, first=first: copies(into, first).start())

    def finish(into):
        for first in range(0, own_unit.shape[0], tile):
            copies(into, first).wait()

    on_target(finish)


scalar = pl.BlockSpec(memory_space=pltpu.SMEM)
on_chip = pl.BlockSpec(memory_space=pltpu.VMEM)
off_chip = pl.BlockSpec(memory_space=pltpu.HBM)
anywhere = pl.BlockSpec(memory_space=pl.ANY)


def pinned(*values):
    return [pltpu.with_memory_space_constraint(value, pltpu.VMEM) for value in values]


def limit(mebibytes):
    return pltpu.CompilerParams(vmem_limit_bytes=mebibytes * 2**20)


def costs(rows, others, width, weight):
    return pl.CostEstimate(
        flops=int(weight * rows * others * width),
        bytes_accessed=4 * rows * width,
        transcendentals=0,
    )


small = pl.CostEstimate(flops=0, bytes_accessed=2**10, transcendentals=0)


def piece_of(images, texts, inner, first, last, tokens):
    raws = [images, texts]
    if not tokens:
        raws = [pltpu.with_memory_space_constraint(raw, pltpu.HBM) for raw in raws]
    return pl.pallas_call(
        functools.partial(piece_kernel, inner, first),
        in_specs=[anywhere if tokens else off_chip] * 2 + [anywhere] * len(tokens),
        out_specs=on_chip,
        out_shape=pltpu.VMEM((last - first, images.shape[1]), images.dtype),
        scratch_shapes=[pltpu.SemaphoreType.DMA],
        compiler_params=limit(1),
        cost_estimate=small,
    )(*raws, *tokens)


def gate(token, *values):
    count = len(values)
    return pl.pallas_call(
        gate_kernel,
        in_specs=[anywhere] + [on_chip] * count,
        out_specs=[on_chip] * count,
        out_shape=[pltpu.VMEM(value.shape, value.dtype) for value in values],
        input_output_aliases={1 + i: i for i in range(count)},
        compiler_params=limit(1),
        cost_estimate=small,
    )(token, *pinned(*values))


def own_block(temper, offset, images, texts):
    rows, width = images.shape
    raws = pltpu.VMEM((rows, width), jnp.bfloat16)
    sums = pltpu.VMEM((rows, width), jnp.float32)
    inverses = pltpu.VMEM((rows, lanes), jnp.float32)
    return pl.pallas_call(
        own_kernel,
        in_specs=[scalar] * 2 + [on_chip] * 2,
        out_specs=[on_chip] * 8,
        out_shape=[raws, raws, sums, sums, raws, raws, inverses, inverses],
        compiler_params=limit(16),
        cost_estimate=costs(rows, rows, width, 32),
    )(temper, offset, *pinned(images, texts))


def more_block(temper, offset, unit, sums, pieces, onward, weight):
    rows, width = unit.shape
    others = sum(piece.shape[0] for piece in pieces)
    return pl.pallas_call(
        functools.partial(more_kernel, len(pieces), onward),
        in_specs=[scalar] * 2 + [on_chip] * (2 + len(pieces)),
        out_specs=[on_chip] * (1 + onward),
        out_shape=[pltpu.VMEM((rows, width), jnp.float32)]
        + [pltpu.VMEM(pieces[-1].shape, jnp.bfloat16)] * onward,
        input_output_aliases={3: 0},
        scratch_shapes=[pltpu.VMEM((others, width), jnp.bfloat16)],
        compiler_params=limit(16),
        cost_estimate=costs(rows, others, width, weight),
    )(temper, offset, *pinned(unit, sums, *pieces))


def last_block(temper, offset, unit, sums, raw, inverse, piece, grads):
    rows, width = unit.shape
    inner = not grads
    return pl.pallas_call(
        functools.partial(last_kernel, inner),
        in_specs=[scalar] * 2 + [on_chip] * 5 + [off_chip] * len(grads),
        out_specs=[off_chip] * 2,
        out_shape=[jax.ShapeDtypeStruct((rows, width), jnp.float32)] * 2,
        input_output_aliases={} if inner else {7: 0, 8: 1},
        scratch_shapes=[
            pltpu.VMEM(piece.shape, jnp.bfloat16),
            pltpu.VMEM((rows, width), jnp.float32),
            pltpu.SemaphoreType.DMA((rows // tile,)),
        ],
        compiler_params=limit(16),
        cost_estimate=costs(rows, piece.shape[0], width, 16),
    )(temper, offset, *pinned(unit, sums, raw, inverse, piece), *grads)


def local(images, texts, log_scale, logit_bias):
    temper = jnp.exp(log_scale)
    rows = images.shape[0]
    near_inner, near_outer = [], []
    tokens = []
    for part in ((0, split), (split, rows)):
        for inner, near in ((True, near_inner), (False, near_outer)):
            piece = piece_of(images, texts, inner, *part, tokens)
            near.append(exchanged(piece, inner))
            tokens = [piece]
    raw_inner, raw_outer, sum_inner, sum_outer, unit_inner, unit_outer, inv_inner, inv_outer = (
        own_block(temper, logit_bias, images, texts)
    )
    near_inner[0], near_outer[0] = gate(inv_inner, near_inner[0], near_outer[0])
    far_outer = exchanged(near_inner[0], False)
    far_inner = exchanged(near_outer[0], True)
    more = functools.partial(more_block, temper, logit_bias)
    near_inner[1], near_outer[1] = gate(inv_inner, near_inner[1], near_outer[1])
    sum_inner, on_inner = more(unit_inner, sum_inner, near_inner, 1, 12)
    sum_outer, on_outer = more(unit_outer, sum_outer, near_outer, 1, 0.01)
    last_outer = exchanged(on_inner, False)
    last_inner = exchanged(on_outer, True)
    (sum_inner,) = more(unit_inner, sum_inner, [far_inner], 0, 0.01)
    (far_outer,) = gate(sum_inner, far_outer)
    (sum_outer,) = more(unit_outer, sum_outer, [far_outer], 0, 0.01)
    (last_inner,) = gate(sum_outer, last_inner)
    last = functools.partial(last_block, temper, logit_bias)
    grads = last(unit_inner, sum_inner, raw_inner, inv_inner, last_inner, ())
    return tuple(last(unit_outer, sum_outer, raw_outer, inv_outer, last_outer, grads))


def solution(mesh):
    return jax.shard_map(
        local,
        mesh=mesh,
        in_specs=(P(axes, None), P(axes, None), P(), P()),
        out_specs=(P(axes, None), P(axes, None)),
        check_vma=False,
    )
```

```python
import functools

import jax
import jax.numpy as jnp
from jax import lax
from jax.experimental import pallas as pl
from jax.experimental.pallas import tpu as pltpu
from jax.sharding import PartitionSpec as P


epsilon = 1e-06
axes = ("grp", "dev")
start = 256
split = 768
tile = 256
lanes = 128


def exchanged(value, inner):
    count = lax.axis_size(axes)
    first = 0 if inner else 1
    pairs = []
    for low in range(first, count, 2):
        high = (low + 1) % count
        pairs += [(low, high), (high, low)]
    return lax.ppermute(value, axes, pairs)


def on_even(is_even, is_odd):
    odd = lax.rem(lax.axis_index("dev"), 2)
    pl.when(odd == 0)(is_even)
    pl.when(odd == 1)(is_odd)


def normalize(raw_rows):
    rows32 = raw_rows.astype(jnp.float32)
    inverse = lax.rsqrt(jnp.sum(rows32 * rows32, axis=1, keepdims=True) + epsilon)
    return rows32 * inverse, inverse


def unit_rows(piece, unit_ref, first=0, inverse_ref=None):
    @pl.loop(0, piece.shape[0] // 128)
    def _(i):
        rows = pl.ds(pl.multiple_of(i * 128, 128), 128)
        into = pl.ds(pl.multiple_of(first + i * 128, 128), 128)
        unit, inverse = normalize(piece[rows, :])
        unit_ref[into, :] = unit.astype(jnp.bfloat16)
        if inverse_ref is not None:
            inverse_ref[into, :] = jnp.broadcast_to(inverse, (128, lanes))


def weigh(own, others, temper, offset, first_row=None):
    logits = (
        temper
        * lax.dot_general(own, others, (((1,), (1,)), ((), ())), preferred_element_type=jnp.float32)
        + offset
    )
    weights = jax.nn.sigmoid(logits)
    if first_row is not None:
        across = lax.broadcasted_iota(jnp.int32, logits.shape, 0) + first_row
        down = lax.broadcasted_iota(jnp.int32, logits.shape, 1)
        weights = weights - jnp.where(across == down, 1.0, 0.0)
    return weights.astype(jnp.bfloat16)


def attend(own_unit, others, temper, offset, sum_ref, finish):
    tiles = [pl.ds(first, tile) for first in range(0, own_unit.shape[0], tile)]
    ahead = weigh(own_unit[tiles[0], :], others[...], temper, offset)
    for rows, following in zip(tiles, tiles[1:] + [None]):
        weights = ahead
        if following is not None:
            ahead = weigh(own_unit[following, :], others[...], temper, offset)
        finish(
            rows,
            sum_ref[rows, :] + jnp.dot(weights, others[...], preferred_element_type=jnp.float32),
        )


def pieces_kernel(first, img_ref, txt_ref, *refs):
    inner_ref, outer_ref, sems = refs[-3:]
    rows = pl.ds(first, inner_ref.shape[0])

    def fetch(*raws):
        copies = [
            pltpu.make_async_copy(raw.at[rows, :], out, sems.at[i])
            for i, (raw, out) in enumerate(zip(raws, (inner_ref, outer_ref)))
        ]
        for copy in copies:
            copy.start()
        for copy in copies:
            copy.wait()

    on_even(lambda: fetch(txt_ref, img_ref), lambda: fetch(img_ref, txt_ref))


def gate_kernel(*refs):
    del refs


def first_kernel(token_ref, inner_ref, outer_ref, inner_unit, outer_unit):
    unit_rows(inner_ref, inner_unit)
    unit_rows(outer_ref, outer_unit)


def rest_kernel(*refs):
    for first_unit, rest, whole, middle, last in (refs[0::2], refs[1::2]):
        count = first_unit.shape[0]
        whole[pl.ds(0, count), :] = first_unit[...]
        unit_rows(rest, whole, count)
        middle[...] = whole[pl.ds(count, middle.shape[0]), :]
        last[...] = whole[pl.ds(count + middle.shape[0], last.shape[0]), :]


def own_kernel(temper_ref, offset_ref, img_ref, txt_ref, *outs):
    raws, sums, units, inverses, sems = outs[:2], outs[2:4], outs[4:6], outs[6:8], outs[8]
    temper, offset = temper_ref[0], offset_ref[0]

    def fetch(*sources):
        copies = [
            pltpu.make_async_copy(source, raw, sems.at[i])
            for i, (source, raw) in enumerate(zip(sources, raws))
        ]
        for copy in copies:
            copy.start()
        for copy in copies:
            copy.wait()

    on_even(lambda: fetch(txt_ref, img_ref), lambda: fetch(img_ref, txt_ref))
    for raw, unit_ref, inverse_ref in zip(raws, units, inverses):
        unit_rows(raw, unit_ref, 0, inverse_ref)

    @pl.loop(0, img_ref.shape[0] // tile)
    def _(i):
        first = pl.multiple_of(i * tile, tile)
        rows = pl.ds(first, tile)
        for side in range(2):
            others = units[1 - side][...]
            weights = weigh(units[side][rows, :], others, temper, offset, first)
            sums[side][rows, :] = jnp.dot(weights, others, preferred_element_type=jnp.float32)


def near_kernel(temper_ref, offset_ref, own_unit, sum_ref, others, out_ref):
    def finish(rows, total):
        out_ref[rows, :] = total

    attend(own_unit, others, temper_ref[0], offset_ref[0], sum_ref, finish)


def far_kernel(temper_ref, offset_ref, own_unit, sum_ref, first, middle, out_ref, others):
    def finish(rows, total):
        out_ref[rows, :] = total

    count = first.shape[0]
    others[pl.ds(0, count), :] = first[...]
    others[pl.ds(count, middle.shape[0]), :] = middle[...]
    attend(own_unit, others, temper_ref[0], offset_ref[0], sum_ref, finish)


def last_kernel(inner, temper_ref, offset_ref, own_unit, sum_ref, raw_ref, inverse_ref, *refs):
    others, *refs = refs if inner else (refs[0], *refs[3:])
    grad_img, grad_txt, ready, sems = refs
    temper = temper_ref[0]

    def copies(into, rows):
        return pltpu.make_async_copy(
            ready.at[rows, :], into.at[rows, :], sems.at[rows.start // tile]
        )

    def on_target(do):
        into_txt, into_img = functools.partial(do, grad_txt), functools.partial(do, grad_img)
        on_even(into_txt, into_img) if inner else on_even(into_img, into_txt)

    def finish(rows, total):
        raw = raw_ref[rows, :].astype(jnp.float32)
        inverse = inverse_ref[rows, :1]
        scale = temper * inverse
        along = jnp.sum(raw * total, axis=1, keepdims=True)
        ready[rows, :] = scale * total - (scale * inverse * inverse * along) * raw
        on_target(lambda into: copies(into, rows).start())

    attend(own_unit, others, temper, offset_ref[0], sum_ref, finish)

    def wait(into):
        for first in range(0, own_unit.shape[0], tile):
            copies(into, pl.ds(first, tile)).wait()

    on_target(wait)


scalar = pl.BlockSpec(memory_space=pltpu.SMEM)
on_chip = pl.BlockSpec(memory_space=pltpu.VMEM)
off_chip = pl.BlockSpec(memory_space=pltpu.HBM)
anywhere = pl.BlockSpec(memory_space=pl.ANY)


def pinned(*values, memory=pltpu.VMEM):
    return [pltpu.with_memory_space_constraint(value, memory) for value in values]


def limit(mebibytes):
    return pltpu.CompilerParams(vmem_limit_bytes=mebibytes * 2**20)


def costs(rows, others, width, weight):
    return pl.CostEstimate(
        flops=int(weight * rows * others * width),
        bytes_accessed=4 * rows * width,
        transcendentals=0,
    )


small = pl.CostEstimate(flops=0, bytes_accessed=2**10, transcendentals=0)


def held(rows, like, dtype=jnp.bfloat16):
    return pltpu.VMEM((rows, like.shape[1]), dtype)


def pieces_of(images, texts, first, last, tokens):
    return pl.pallas_call(
        functools.partial(pieces_kernel, first),
        in_specs=[off_chip] * 2 + [anywhere] * len(tokens),
        out_specs=[on_chip] * 2,
        out_shape=[held(last - first, images)] * 2,
        scratch_shapes=[pltpu.SemaphoreType.DMA((2,))],
        compiler_params=limit(1),
        cost_estimate=small,
    )(*pinned(images, texts, memory=pltpu.HBM), *tokens)


def first_units(token, inner, outer):
    return pl.pallas_call(
        first_kernel,
        in_specs=[anywhere] + [on_chip] * 2,
        out_specs=[on_chip] * 2,
        out_shape=[held(inner.shape[0], inner)] * 2,
        compiler_params=limit(4),
        cost_estimate=small,
    )(token, *pinned(inner, outer))


def rest_units(firsts, rests):
    count, width = firsts[0].shape[0], firsts[0]
    more = rests[0].shape[0]
    sizes = (count + more, split - count, count + more - split)
    return pl.pallas_call(
        rest_kernel,
        in_specs=[on_chip] * 4,
        out_specs=[on_chip] * 6,
        out_shape=[held(size, width) for size in sizes for _ in range(2)],
        compiler_params=limit(4),
        cost_estimate=small,
    )(*pinned(*firsts, *rests))


def gate(token, *values):
    count = len(values)
    return pl.pallas_call(
        gate_kernel,
        in_specs=[anywhere] + [on_chip] * count,
        out_specs=[on_chip] * count,
        out_shape=[pltpu.VMEM(value.shape, value.dtype) for value in values],
        input_output_aliases={1 + i: i for i in range(count)},
        compiler_params=limit(1),
        cost_estimate=small,
    )(token, *pinned(*values))


def own_block(temper, offset, images, texts):
    rows = images.shape[0]
    raws, sums = held(rows, images), held(rows, images, jnp.float32)
    inverses = pltpu.VMEM((rows, lanes), jnp.float32)
    return pl.pallas_call(
        own_kernel,
        in_specs=[scalar] * 2 + [off_chip] * 2,
        out_specs=[on_chip] * 8,
        out_shape=[raws, raws, sums, sums, raws, raws, inverses, inverses],
        scratch_shapes=[pltpu.SemaphoreType.DMA((2,))],
        compiler_params=limit(16),
        cost_estimate=costs(rows, rows, images.shape[1], 32),
    )(temper, offset, *pinned(images, texts, memory=pltpu.HBM))


def more_block(temper, offset, unit, sums, pieces, weight):
    rows, width = unit.shape
    others = sum(piece.shape[0] for piece in pieces)
    several = len(pieces) > 1
    return pl.pallas_call(
        far_kernel if several else near_kernel,
        in_specs=[scalar] * 2 + [on_chip] * (2 + len(pieces)),
        out_specs=on_chip,
        out_shape=held(rows, unit, jnp.float32),
        input_output_aliases={3: 0},
        scratch_shapes=[pltpu.VMEM((others, width), jnp.bfloat16)] * several,
        compiler_params=limit(16),
        cost_estimate=costs(rows, others, width, weight),
    )(temper, offset, *pinned(unit, sums, *pieces))


def last_block(temper, offset, unit, sums, raw, inverse, piece, grads):
    rows, width = unit.shape
    inner = not grads
    return pl.pallas_call(
        functools.partial(last_kernel, inner),
        in_specs=[scalar] * 2 + [on_chip] * 5 + [off_chip] * len(grads),
        out_specs=[off_chip] * 2,
        out_shape=[jax.ShapeDtypeStruct((rows, width), jnp.float32)] * 2,
        input_output_aliases={} if inner else {7: 0, 8: 1},
        scratch_shapes=[
            pltpu.VMEM((rows, width), jnp.float32),
            pltpu.SemaphoreType.DMA((rows // tile,)),
        ],
        compiler_params=limit(16),
        cost_estimate=costs(rows, piece.shape[0], width, 16),
    )(temper, offset, *pinned(unit, sums, raw, inverse, piece), *grads)


def local(images, texts, log_scale, logit_bias):
    temper = jnp.exp(log_scale)
    rows = images.shape[0]
    pieces = pieces_of(images, texts, 0, start, [])
    pieces = [pieces[0], gate(pieces[0], pieces[1])[0]]
    firsts = [exchanged(pieces[0], True), exchanged(pieces[1], False)]
    pieces = pieces_of(images, texts, start, rows, pieces[:1])
    rests = [exchanged(pieces[0], True), exchanged(pieces[1], False)]
    raw_inner, raw_outer, sum_inner, sum_outer, unit_inner, unit_outer, inv_inner, inv_outer = (
        own_block(temper, logit_bias, images, texts)
    )
    firsts = first_units(inv_inner, *firsts)
    far_outer, far_inner = exchanged(firsts[0], False), exchanged(firsts[1], True)
    near_inner, near_outer, *middles, last_inner, last_outer = rest_units(firsts, rests)
    middle_outer, middle_inner = exchanged(middles[0], False), exchanged(middles[1], True)
    more = functools.partial(more_block, temper, logit_bias)
    sum_inner = more(unit_inner, sum_inner, [near_inner], 6)
    sum_outer = more(unit_outer, sum_outer, [near_outer], 6)
    last_inner, last_outer, far_inner, far_outer = gate(
        sum_outer, last_inner, last_outer, far_inner, far_outer
    )
    last_outer, last_inner = exchanged(last_inner, False), exchanged(last_outer, True)
    sum_inner = more(unit_inner, sum_inner, [far_inner, middle_inner], 0.01)
    (middle_outer,) = gate(sum_inner, middle_outer)
    sum_outer = more(unit_outer, sum_outer, [far_outer, middle_outer], 0.01)
    (last_inner,) = gate(sum_outer, last_inner)
    last = functools.partial(last_block, temper, logit_bias)
    grads = last(unit_inner, sum_inner, raw_inner, inv_inner, last_inner, ())
    return tuple(last(unit_outer, sum_outer, raw_outer, inv_outer, last_outer, grads))


def solution(mesh):
    return jax.shard_map(
        local,
        mesh=mesh,
        in_specs=(P(axes, None), P(axes, None), P(), P()),
        out_specs=(P(axes, None), P(axes, None)),
        check_vma=False,
    )
```

```python
import functools

import jax
import jax.numpy as jnp
from jax import lax
from jax.experimental import pallas as pl
from jax.experimental.pallas import tpu as pltpu
from jax.sharding import PartitionSpec as P


epsilon = 1e-06
axes = ("grp", "dev")
start = 256
split = 768
tile = 256
last_tiles = (128, 256, 256, 256, 128)
lanes = 128


def exchanged(value, inner):
    count = lax.axis_size(axes)
    first = 0 if inner else 1
    pairs = []
    for low in range(first, count, 2):
        high = (low + 1) % count
        pairs += [(low, high), (high, low)]
    return lax.ppermute(value, axes, pairs)


def passed_along(value, steps):
    count = lax.axis_size(axes)
    pairs = [(source, (source + steps) % count) for source in range(count)]
    return lax.ppermute(value, axes, pairs)


def on_even(is_even, is_odd):
    odd = lax.rem(lax.axis_index("dev"), 2)
    pl.when(odd == 0)(is_even)
    pl.when(odd == 1)(is_odd)


def normalize(raw_rows):
    rows32 = raw_rows.astype(jnp.float32)
    inverse = lax.rsqrt(jnp.sum(rows32 * rows32, axis=1, keepdims=True) + epsilon)
    return rows32 * inverse, inverse


def unit_rows(piece, unit_ref, first=0, inverse_ref=None):
    @pl.loop(0, piece.shape[0] // 128)
    def _(i):
        rows = pl.ds(pl.multiple_of(i * 128, 128), 128)
        into = pl.ds(pl.multiple_of(first + i * 128, 128), 128)
        unit, inverse = normalize(piece[rows, :])
        unit_ref[into, :] = unit.astype(jnp.bfloat16)
        if inverse_ref is not None:
            inverse_ref[into, :] = jnp.broadcast_to(inverse, (128, lanes))


def weigh(own, others, temper, offset, first_row=None):
    logits = (
        temper
        * lax.dot_general(own, others, (((1,), (1,)), ((), ())), preferred_element_type=jnp.float32)
        + offset
    )
    weights = jax.nn.sigmoid(logits)
    if first_row is not None:
        across = lax.broadcasted_iota(jnp.int32, logits.shape, 0) + first_row
        down = lax.broadcasted_iota(jnp.int32, logits.shape, 1)
        weights = weights - jnp.where(across == down, 1.0, 0.0)
    return weights.astype(jnp.bfloat16)


def attend(own_unit, others, temper, offset, sum_ref, finish, sizes=(tile,) * 4):
    tiles = [pl.ds(sum(sizes[:i]), size) for i, size in enumerate(sizes)]
    ahead = weigh(own_unit[tiles[0], :], others[...], temper, offset)
    for rows, following in zip(tiles, tiles[1:] + [None]):
        weights = ahead
        if following is not None:
            ahead = weigh(own_unit[following, :], others[...], temper, offset)
        finish(
            rows,
            sum_ref[rows, :] + jnp.dot(weights, others[...], preferred_element_type=jnp.float32),
        )


def pieces_kernel(first, by_name, img_ref, txt_ref, *refs):
    inner_ref, outer_ref, sems = refs[-3:]
    rows = pl.ds(first, inner_ref.shape[0])

    def fetch(*raws):
        copies = [
            pltpu.make_async_copy(raw.at[rows, :], out, sems.at[i])
            for i, (raw, out) in enumerate(zip(raws, (inner_ref, outer_ref)))
        ]
        for copy in copies:
            copy.start()
        for copy in copies:
            copy.wait()

    if by_name:
        on_even(lambda: fetch(txt_ref, img_ref), lambda: fetch(img_ref, txt_ref))
    else:
        fetch(txt_ref, img_ref)


def gate_kernel(*refs):
    del refs


def first_kernel(token_ref, txt_ref, img_ref, inner_unit, outer_unit):
    def take(inner_ref, outer_ref):
        unit_rows(inner_ref, inner_unit)
        unit_rows(outer_ref, outer_unit)

    on_even(lambda: take(img_ref, txt_ref), lambda: take(txt_ref, img_ref))


def rest_kernel(*refs):
    for first_unit, rest, whole, middle, last in (refs[0::2], refs[1::2]):
        count = first_unit.shape[0]
        whole[pl.ds(0, count), :] = first_unit[...]
        unit_rows(rest, whole, count)
        middle[...] = whole[pl.ds(count, middle.shape[0]), :]
        last[...] = whole[pl.ds(count + middle.shape[0], last.shape[0]), :]


def own_kernel(temper_ref, offset_ref, img_ref, txt_ref, *outs):
    raws, sums, units, inverses, sems = outs[:2], outs[2:4], outs[4:6], outs[6:8], outs[8]
    temper, offset = temper_ref[0], offset_ref[0]

    def fetch(*sources):
        copies = [
            pltpu.make_async_copy(source, raw, sems.at[i])
            for i, (source, raw) in enumerate(zip(sources, raws))
        ]
        for copy in copies:
            copy.start()
        for copy in copies:
            copy.wait()

    on_even(lambda: fetch(txt_ref, img_ref), lambda: fetch(img_ref, txt_ref))
    for raw, unit_ref, inverse_ref in zip(raws, units, inverses):
        unit_rows(raw, unit_ref, 0, inverse_ref)

    @pl.loop(0, img_ref.shape[0] // tile)
    def _(i):
        first = pl.multiple_of(i * tile, tile)
        rows = pl.ds(first, tile)
        for side in range(2):
            others = units[1 - side][...]
            weights = weigh(units[side][rows, :], others, temper, offset, first)
            sums[side][rows, :] = jnp.dot(weights, others, preferred_element_type=jnp.float32)


def near_kernel(temper_ref, offset_ref, own_unit, sum_ref, others, out_ref):
    def finish(rows, total):
        out_ref[rows, :] = total

    attend(own_unit, others, temper_ref[0], offset_ref[0], sum_ref, finish)


def far_kernel(temper_ref, offset_ref, own_unit, sum_ref, first, middle, out_ref, others):
    def finish(rows, total):
        out_ref[rows, :] = total

    count = first.shape[0]
    others[pl.ds(0, count), :] = first[...]
    others[pl.ds(count, middle.shape[0]), :] = middle[...]
    attend(own_unit, others, temper_ref[0], offset_ref[0], sum_ref, finish)


def last_kernel(inner, temper_ref, offset_ref, own_unit, sum_ref, raw_ref, inverse_ref, *refs):
    others, *refs = refs if inner else (refs[0], *refs[3:])
    grad_img, grad_txt, ready, sems = refs
    temper = temper_ref[0]

    def run(into):
        copies = []

        def finish(rows, total):
            raw = raw_ref[rows, :].astype(jnp.float32)
            inverse = inverse_ref[rows, :1]
            scale = temper * inverse
            along = jnp.sum(raw * total, axis=1, keepdims=True)
            ready[rows, :] = scale * total - (scale * inverse * inverse * along) * raw
            copies.append(
                pltpu.make_async_copy(ready.at[rows, :], into.at[rows, :], sems.at[len(copies)])
            )
            copies[-1].start()

        attend(own_unit, others, temper, offset_ref[0], sum_ref, finish, last_tiles)
        for copy in copies:
            copy.wait()

    into_txt, into_img = functools.partial(run, grad_txt), functools.partial(run, grad_img)
    on_even(into_txt, into_img) if inner else on_even(into_img, into_txt)


scalar = pl.BlockSpec(memory_space=pltpu.SMEM)
on_chip = pl.BlockSpec(memory_space=pltpu.VMEM)
off_chip = pl.BlockSpec(memory_space=pltpu.HBM)
anywhere = pl.BlockSpec(memory_space=pl.ANY)


def pinned(*values, memory=pltpu.VMEM):
    return [pltpu.with_memory_space_constraint(value, memory) for value in values]


def limit(mebibytes):
    return pltpu.CompilerParams(vmem_limit_bytes=mebibytes * 2**20)


def costs(rows, others, width, weight):
    return pl.CostEstimate(
        flops=int(weight * rows * others * width),
        bytes_accessed=4 * rows * width,
        transcendentals=0,
    )


small = pl.CostEstimate(flops=0, bytes_accessed=2**10, transcendentals=0)


def held(rows, like, dtype=jnp.bfloat16):
    return pltpu.VMEM((rows, like.shape[1]), dtype)


def pieces_of(images, texts, first, last, tokens):
    return pl.pallas_call(
        functools.partial(pieces_kernel, first, bool(tokens)),
        in_specs=[off_chip] * 2 + [anywhere] * len(tokens),
        out_specs=[on_chip] * 2,
        out_shape=[held(last - first, images)] * 2,
        scratch_shapes=[pltpu.SemaphoreType.DMA((2,))],
        compiler_params=limit(1),
        cost_estimate=small,
    )(*pinned(images, texts, memory=pltpu.HBM), *tokens)


def first_units(token, texts, images):
    return pl.pallas_call(
        first_kernel,
        in_specs=[anywhere] + [on_chip] * 2,
        out_specs=[on_chip] * 2,
        out_shape=[held(texts.shape[0], texts)] * 2,
        compiler_params=limit(4),
        cost_estimate=small,
    )(token, *pinned(texts, images))


def rest_units(firsts, rests):
    count, width = firsts[0].shape[0], firsts[0]
    more = rests[0].shape[0]
    sizes = (count + more, split - count, count + more - split)
    return pl.pallas_call(
        rest_kernel,
        in_specs=[on_chip] * 4,
        out_specs=[on_chip] * 6,
        out_shape=[held(size, width) for size in sizes for _ in range(2)],
        compiler_params=limit(4),
        cost_estimate=small,
    )(*pinned(*firsts, *rests))


def gate(token, *values):
    count = len(values)
    return pl.pallas_call(
        gate_kernel,
        in_specs=[anywhere] + [on_chip] * count,
        out_specs=[on_chip] * count,
        out_shape=[pltpu.VMEM(value.shape, value.dtype) for value in values],
        input_output_aliases={1 + i: i for i in range(count)},
        compiler_params=limit(1),
        cost_estimate=small,
    )(token, *pinned(*values))


def own_block(temper, offset, images, texts):
    rows = images.shape[0]
    raws, sums = held(rows, images), held(rows, images, jnp.float32)
    inverses = pltpu.VMEM((rows, lanes), jnp.float32)
    return pl.pallas_call(
        own_kernel,
        in_specs=[scalar] * 2 + [off_chip] * 2,
        out_specs=[on_chip] * 8,
        out_shape=[raws, raws, sums, sums, raws, raws, inverses, inverses],
        scratch_shapes=[pltpu.SemaphoreType.DMA((2,))],
        compiler_params=limit(16),
        cost_estimate=costs(rows, rows, images.shape[1], 32),
    )(temper, offset, *pinned(images, texts, memory=pltpu.HBM))


def more_block(temper, offset, unit, sums, pieces, weight):
    rows, width = unit.shape
    others = sum(piece.shape[0] for piece in pieces)
    several = len(pieces) > 1
    return pl.pallas_call(
        far_kernel if several else near_kernel,
        in_specs=[scalar] * 2 + [on_chip] * (2 + len(pieces)),
        out_specs=on_chip,
        out_shape=held(rows, unit, jnp.float32),
        input_output_aliases={3: 0},
        scratch_shapes=[pltpu.VMEM((others, width), jnp.bfloat16)] * several,
        compiler_params=limit(16),
        cost_estimate=costs(rows, others, width, weight),
    )(temper, offset, *pinned(unit, sums, *pieces))


def last_block(temper, offset, unit, sums, raw, inverse, piece, grads):
    rows, width = unit.shape
    inner = not grads
    return pl.pallas_call(
        functools.partial(last_kernel, inner),
        in_specs=[scalar] * 2 + [on_chip] * 5 + [off_chip] * len(grads),
        out_specs=[off_chip] * 2,
        out_shape=[jax.ShapeDtypeStruct((rows, width), jnp.float32)] * 2,
        input_output_aliases={} if inner else {7: 0, 8: 1},
        scratch_shapes=[
            pltpu.VMEM((rows, width), jnp.float32),
            pltpu.SemaphoreType.DMA((len(last_tiles),)),
        ],
        compiler_params=limit(16),
        cost_estimate=costs(rows, piece.shape[0], width, 16),
    )(temper, offset, *pinned(unit, sums, raw, inverse, piece), *grads)


def local(images, texts, log_scale, logit_bias):
    temper = jnp.exp(log_scale)
    rows = images.shape[0]
    pieces = pieces_of(images, texts, 0, start, [])
    pieces = [pieces[0], gate(pieces[0], pieces[1])[0]]
    firsts = [passed_along(pieces[0], 1), passed_along(pieces[1], -1)]
    pieces = pieces_of(images, texts, start, rows, pieces[:1])
    rests = [exchanged(pieces[0], True), exchanged(pieces[1], False)]
    raw_inner, raw_outer, sum_inner, sum_outer, unit_inner, unit_outer, inv_inner, inv_outer = (
        own_block(temper, logit_bias, images, texts)
    )
    firsts = first_units(inv_inner, *firsts)
    far_outer, far_inner = exchanged(firsts[0], False), exchanged(firsts[1], True)
    near_inner, near_outer, *middles, last_inner, last_outer = rest_units(firsts, rests)
    middle_outer, middle_inner = exchanged(middles[0], False), exchanged(middles[1], True)
    more = functools.partial(more_block, temper, logit_bias)
    sum_inner = more(unit_inner, sum_inner, [near_inner], 6)
    sum_outer = more(unit_outer, sum_outer, [near_outer], 6)
    last_inner, last_outer, far_inner, far_outer = gate(
        sum_outer, last_inner, last_outer, far_inner, far_outer
    )
    last_outer, last_inner = exchanged(last_inner, False), exchanged(last_outer, True)
    sum_inner = more(unit_inner, sum_inner, [far_inner, middle_inner], 0.01)
    (middle_outer,) = gate(sum_inner, middle_outer)
    sum_outer = more(unit_outer, sum_outer, [far_outer, middle_outer], 0.01)
    (last_inner,) = gate(sum_outer, last_inner)
    last = functools.partial(last_block, temper, logit_bias)
    grads = last(unit_inner, sum_inner, raw_inner, inv_inner, last_inner, ())
    return tuple(last(unit_outer, sum_outer, raw_outer, inv_outer, last_outer, grads))


def solution(mesh):
    return jax.shard_map(
        local,
        mesh=mesh,
        in_specs=(P(axes, None), P(axes, None), P(), P()),
        out_specs=(P(axes, None), P(axes, None)),
        check_vma=False,
    )
```

```python
import functools

import jax
import jax.numpy as jnp
from jax import lax
from jax.experimental import pallas as pl
from jax.experimental.pallas import tpu as pltpu
from jax.sharding import PartitionSpec as P


epsilon = 1e-06
axes = ("grp", "dev")
start = 256
split = 768
tile = 256
last_tiles = (128, 256, 256, 256, 128)
lanes = 128


def exchanged(value, inner):
    count = lax.axis_size(axes)
    first = 0 if inner else 1
    pairs = []
    for low in range(first, count, 2):
        high = (low + 1) % count
        pairs += [(low, high), (high, low)]
    return lax.ppermute(value, axes, pairs)


def on_even(is_even, is_odd):
    odd = lax.rem(lax.axis_index("dev"), 2)
    pl.when(odd == 0)(is_even)
    pl.when(odd == 1)(is_odd)


def normalize(raw_rows):
    rows32 = raw_rows.astype(jnp.float32)
    inverse = lax.rsqrt(jnp.sum(rows32 * rows32, axis=1, keepdims=True) + epsilon)
    return rows32 * inverse, inverse


def unit_rows(piece, unit_ref, first=0, inverse_ref=None):
    @pl.loop(0, piece.shape[0] // 128)
    def _(i):
        rows = pl.ds(pl.multiple_of(i * 128, 128), 128)
        into = pl.ds(pl.multiple_of(first + i * 128, 128), 128)
        unit, inverse = normalize(piece[rows, :])
        unit_ref[into, :] = unit.astype(jnp.bfloat16)
        if inverse_ref is not None:
            inverse_ref[into, :] = jnp.broadcast_to(inverse, (128, lanes))


def weigh(own, others, temper, offset, first_row=None):
    logits = (
        temper
        * lax.dot_general(own, others, (((1,), (1,)), ((), ())), preferred_element_type=jnp.float32)
        + offset
    )
    weights = jax.nn.sigmoid(logits)
    if first_row is not None:
        across = lax.broadcasted_iota(jnp.int32, logits.shape, 0) + first_row
        down = lax.broadcasted_iota(jnp.int32, logits.shape, 1)
        weights = weights - jnp.where(across == down, 1.0, 0.0)
    return weights.astype(jnp.bfloat16)


def attend(own_unit, others, temper, offset, sum_ref, finish, sizes=(tile,) * 4):
    tiles = [pl.ds(sum(sizes[:i]), size) for i, size in enumerate(sizes)]
    ahead = weigh(own_unit[tiles[0], :], others[...], temper, offset)
    for rows, following in zip(tiles, tiles[1:] + [None]):
        weights = ahead
        if following is not None:
            ahead = weigh(own_unit[following, :], others[...], temper, offset)
        finish(
            rows,
            sum_ref[rows, :] + jnp.dot(weights, others[...], preferred_element_type=jnp.float32),
        )


def pieces_kernel(first, img_ref, txt_ref, *refs):
    inner_ref, outer_ref, sems = refs[-3:]
    rows = pl.ds(first, inner_ref.shape[0])

    def fetch(*raws):
        copies = [
            pltpu.make_async_copy(raw.at[rows, :], out, sems.at[i])
            for i, (raw, out) in enumerate(zip(raws, (inner_ref, outer_ref)))
        ]
        for copy in copies:
            copy.start()
        for copy in copies:
            copy.wait()

    on_even(lambda: fetch(txt_ref, img_ref), lambda: fetch(img_ref, txt_ref))


def gate_kernel(*refs):
    del refs


def first_kernel(token_ref, inner_ref, outer_ref, inner_unit, outer_unit):
    unit_rows(inner_ref, inner_unit)
    unit_rows(outer_ref, outer_unit)


def rest_kernel(*refs):
    for first_unit, rest, whole, middle, last in (refs[0::2], refs[1::2]):
        count = first_unit.shape[0]
        whole[pl.ds(0, count), :] = first_unit[...]
        unit_rows(rest, whole, count)
        middle[...] = whole[pl.ds(count, middle.shape[0]), :]
        last[...] = whole[pl.ds(count + middle.shape[0], last.shape[0]), :]


def own_kernel(temper_ref, offset_ref, img_ref, txt_ref, *outs):
    raws, sums, units, inverses, sems = outs[:2], outs[2:4], outs[4:6], outs[6:8], outs[8]
    temper, offset = temper_ref[0], offset_ref[0]

    def fetch(*sources):
        copies = [
            pltpu.make_async_copy(source, raw, sems.at[i])
            for i, (source, raw) in enumerate(zip(sources, raws))
        ]
        for copy in copies:
            copy.start()
        for copy in copies:
            copy.wait()

    on_even(lambda: fetch(txt_ref, img_ref), lambda: fetch(img_ref, txt_ref))
    for raw, unit_ref, inverse_ref in zip(raws, units, inverses):
        unit_rows(raw, unit_ref, 0, inverse_ref)

    @pl.loop(0, img_ref.shape[0] // tile)
    def _(i):
        first = pl.multiple_of(i * tile, tile)
        rows = pl.ds(first, tile)
        for side in range(2):
            others = units[1 - side][...]
            weights = weigh(units[side][rows, :], others, temper, offset, first)
            sums[side][rows, :] = jnp.dot(weights, others, preferred_element_type=jnp.float32)


def near_kernel(temper_ref, offset_ref, own_unit, sum_ref, others, out_ref):
    def finish(rows, total):
        out_ref[rows, :] = total

    attend(own_unit, others, temper_ref[0], offset_ref[0], sum_ref, finish)


def far_kernel(temper_ref, offset_ref, own_unit, sum_ref, first, middle, out_ref, others):
    def finish(rows, total):
        out_ref[rows, :] = total

    count = first.shape[0]
    others[pl.ds(0, count), :] = first[...]
    others[pl.ds(count, middle.shape[0]), :] = middle[...]
    attend(own_unit, others, temper_ref[0], offset_ref[0], sum_ref, finish)


def last_kernel(inner, temper_ref, offset_ref, own_unit, sum_ref, raw_ref, inverse_ref, *refs):
    others, *refs = refs if inner else (refs[0], *refs[3:])
    grad_img, grad_txt, ready, sems = refs
    temper = temper_ref[0]

    def run(into):
        copies = []

        def finish(rows, total):
            raw = raw_ref[rows, :].astype(jnp.float32)
            inverse = inverse_ref[rows, :1]
            scale = temper * inverse
            along = jnp.sum(raw * total, axis=1, keepdims=True)
            ready[rows, :] = scale * total - (scale * inverse * inverse * along) * raw
            copies.append(
                pltpu.make_async_copy(ready.at[rows, :], into.at[rows, :], sems.at[len(copies)])
            )
            copies[-1].start()

        attend(own_unit, others, temper, offset_ref[0], sum_ref, finish, last_tiles)
        for copy in copies:
            copy.wait()

    into_txt, into_img = functools.partial(run, grad_txt), functools.partial(run, grad_img)
    on_even(into_txt, into_img) if inner else on_even(into_img, into_txt)


scalar = pl.BlockSpec(memory_space=pltpu.SMEM)
on_chip = pl.BlockSpec(memory_space=pltpu.VMEM)
off_chip = pl.BlockSpec(memory_space=pltpu.HBM)
anywhere = pl.BlockSpec(memory_space=pl.ANY)


def pinned(*values, memory=pltpu.VMEM):
    return [pltpu.with_memory_space_constraint(value, memory) for value in values]


def limit(mebibytes):
    return pltpu.CompilerParams(vmem_limit_bytes=mebibytes * 2**20)


def costs(rows, others, width, weight):
    return pl.CostEstimate(
        flops=int(weight * rows * others * width),
        bytes_accessed=4 * rows * width,
        transcendentals=0,
    )


small = pl.CostEstimate(flops=0, bytes_accessed=2**10, transcendentals=0)


def held(rows, like, dtype=jnp.bfloat16):
    return pltpu.VMEM((rows, like.shape[1]), dtype)


def pieces_of(images, texts, first, last, tokens):
    return pl.pallas_call(
        functools.partial(pieces_kernel, first),
        in_specs=[off_chip] * 2 + [anywhere] * len(tokens),
        out_specs=[on_chip] * 2,
        out_shape=[held(last - first, images)] * 2,
        scratch_shapes=[pltpu.SemaphoreType.DMA((2,))],
        compiler_params=limit(1),
        cost_estimate=small,
    )(*pinned(images, texts, memory=pltpu.HBM), *tokens)


def first_units(token, inner, outer):
    return pl.pallas_call(
        first_kernel,
        in_specs=[anywhere] + [on_chip] * 2,
        out_specs=[on_chip] * 2,
        out_shape=[held(inner.shape[0], inner)] * 2,
        compiler_params=limit(4),
        cost_estimate=small,
    )(token, *pinned(inner, outer))


def rest_units(firsts, rests):
    count, width = firsts[0].shape[0], firsts[0]
    more = rests[0].shape[0]
    sizes = (count + more, split - count, count + more - split)
    return pl.pallas_call(
        rest_kernel,
        in_specs=[on_chip] * 4,
        out_specs=[on_chip] * 6,
        out_shape=[held(size, width) for size in sizes for _ in range(2)],
        compiler_params=limit(4),
        cost_estimate=small,
    )(*pinned(*firsts, *rests))


def gate(token, *values):
    count = len(values)
    return pl.pallas_call(
        gate_kernel,
        in_specs=[anywhere] + [on_chip] * count,
        out_specs=[on_chip] * count,
        out_shape=[pltpu.VMEM(value.shape, value.dtype) for value in values],
        input_output_aliases={1 + i: i for i in range(count)},
        compiler_params=limit(1),
        cost_estimate=small,
    )(token, *pinned(*values))


def own_block(temper, offset, images, texts):
    rows = images.shape[0]
    raws, sums = held(rows, images), held(rows, images, jnp.float32)
    inverses = pltpu.VMEM((rows, lanes), jnp.float32)
    return pl.pallas_call(
        own_kernel,
        in_specs=[scalar] * 2 + [off_chip] * 2,
        out_specs=[on_chip] * 8,
        out_shape=[raws, raws, sums, sums, raws, raws, inverses, inverses],
        scratch_shapes=[pltpu.SemaphoreType.DMA((2,))],
        compiler_params=limit(16),
        cost_estimate=costs(rows, rows, images.shape[1], 32),
    )(temper, offset, *pinned(images, texts, memory=pltpu.HBM))


def more_block(temper, offset, unit, sums, pieces, weight):
    rows, width = unit.shape
    others = sum(piece.shape[0] for piece in pieces)
    several = len(pieces) > 1
    return pl.pallas_call(
        far_kernel if several else near_kernel,
        in_specs=[scalar] * 2 + [on_chip] * (2 + len(pieces)),
        out_specs=on_chip,
        out_shape=held(rows, unit, jnp.float32),
        input_output_aliases={3: 0},
        scratch_shapes=[pltpu.VMEM((others, width), jnp.bfloat16)] * several,
        compiler_params=limit(16),
        cost_estimate=costs(rows, others, width, weight),
    )(temper, offset, *pinned(unit, sums, *pieces))


def last_block(temper, offset, unit, sums, raw, inverse, piece, grads):
    rows, width = unit.shape
    inner = not grads
    return pl.pallas_call(
        functools.partial(last_kernel, inner),
        in_specs=[scalar] * 2 + [on_chip] * 5 + [off_chip] * len(grads),
        out_specs=[off_chip] * 2,
        out_shape=[jax.ShapeDtypeStruct((rows, width), jnp.float32)] * 2,
        input_output_aliases={} if inner else {7: 0, 8: 1},
        scratch_shapes=[
            pltpu.VMEM((rows, width), jnp.float32),
            pltpu.SemaphoreType.DMA((len(last_tiles),)),
        ],
        compiler_params=limit(16),
        cost_estimate=costs(rows, piece.shape[0], width, 16),
    )(temper, offset, *pinned(unit, sums, raw, inverse, piece), *grads)


def local(images, texts, log_scale, logit_bias):
    temper = jnp.exp(log_scale)
    rows = images.shape[0]
    pieces = pieces_of(images, texts, 0, start, [])
    pieces = [pieces[0], gate(pieces[0], pieces[1])[0]]
    firsts = [exchanged(pieces[0], True), exchanged(pieces[1], False)]
    pieces = pieces_of(images, texts, start, rows, pieces[:1])
    rests = [exchanged(pieces[0], True), exchanged(pieces[1], False)]
    raw_inner, raw_outer, sum_inner, sum_outer, unit_inner, unit_outer, inv_inner, inv_outer = (
        own_block(temper, logit_bias, images, texts)
    )
    firsts = first_units(inv_inner, *firsts)
    far_outer, far_inner = exchanged(firsts[0], False), exchanged(firsts[1], True)
    near_inner, near_outer, *middles, last_inner, last_outer = rest_units(firsts, rests)
    middle_outer, middle_inner = exchanged(middles[0], False), exchanged(middles[1], True)
    more = functools.partial(more_block, temper, logit_bias)
    sum_inner = more(unit_inner, sum_inner, [near_inner], 6)
    sum_outer = more(unit_outer, sum_outer, [near_outer], 6)
    last_inner, last_outer, far_inner, far_outer = gate(
        sum_outer, last_inner, last_outer, far_inner, far_outer
    )
    last_outer, last_inner = exchanged(last_inner, False), exchanged(last_outer, True)
    sum_inner = more(unit_inner, sum_inner, [far_inner, middle_inner], 0.01)
    (middle_outer,) = gate(sum_inner, middle_outer)
    sum_outer = more(unit_outer, sum_outer, [far_outer, middle_outer], 0.01)
    (last_inner,) = gate(sum_outer, last_inner)
    last = functools.partial(last_block, temper, logit_bias)
    grads = last(unit_inner, sum_inner, raw_inner, inv_inner, last_inner, ())
    return tuple(last(unit_outer, sum_outer, raw_outer, inv_outer, last_outer, grads))


def solution(mesh):
    return jax.shard_map(
        local,
        mesh=mesh,
        in_specs=(P(axes, None), P(axes, None), P(), P()),
        out_specs=(P(axes, None), P(axes, None)),
        check_vma=False,
    )
```

```python
import functools

import jax
import jax.numpy as jnp
from jax import lax
from jax.experimental import pallas as pl
from jax.experimental.pallas import tpu as pltpu
from jax.sharding import PartitionSpec as P


epsilon = 1e-06
axes = ("grp", "dev")
start = 256
split = 832
tile = 256
last_tiles = (128, 256, 256, 256, 64, 64)
lanes = 128


def exchanged(value, inner):
    count = lax.axis_size(axes)
    first = 0 if inner else 1
    pairs = []
    for low in range(first, count, 2):
        high = (low + 1) % count
        pairs += [(low, high), (high, low)]
    return lax.ppermute(value, axes, pairs)


def on_even(is_even, is_odd):
    odd = lax.rem(lax.axis_index("dev"), 2)
    pl.when(odd == 0)(is_even)
    pl.when(odd == 1)(is_odd)


def normalize(raw_rows):
    rows32 = raw_rows.astype(jnp.float32)
    inverse = lax.rsqrt(jnp.sum(rows32 * rows32, axis=1, keepdims=True) + epsilon)
    return rows32 * inverse, inverse


def unit_rows(piece, unit_ref, first=0, inverse_ref=None):
    @pl.loop(0, piece.shape[0] // 128)
    def _(i):
        rows = pl.ds(pl.multiple_of(i * 128, 128), 128)
        into = pl.ds(pl.multiple_of(first + i * 128, 128), 128)
        unit, inverse = normalize(piece[rows, :])
        unit_ref[into, :] = unit.astype(jnp.bfloat16)
        if inverse_ref is not None:
            inverse_ref[into, :] = jnp.broadcast_to(inverse, (128, lanes))


def weigh(own, others, temper, offset, first_row=None):
    logits = (
        temper
        * lax.dot_general(own, others, (((1,), (1,)), ((), ())), preferred_element_type=jnp.float32)
        + offset
    )
    weights = jax.nn.sigmoid(logits)
    if first_row is not None:
        across = lax.broadcasted_iota(jnp.int32, logits.shape, 0) + first_row
        down = lax.broadcasted_iota(jnp.int32, logits.shape, 1)
        weights = weights - jnp.where(across == down, 1.0, 0.0)
    return weights.astype(jnp.bfloat16)


def attend(own_unit, others, temper, offset, sum_ref, finish, sizes=(tile,) * 4):
    tiles = [pl.ds(sum(sizes[:i]), size) for i, size in enumerate(sizes)]
    ahead = weigh(own_unit[tiles[0], :], others[...], temper, offset)
    for rows, following in zip(tiles, tiles[1:] + [None]):
        weights = ahead
        if following is not None:
            ahead = weigh(own_unit[following, :], others[...], temper, offset)
        finish(
            rows,
            sum_ref[rows, :] + jnp.dot(weights, others[...], preferred_element_type=jnp.float32),
        )


def pieces_kernel(first, img_ref, txt_ref, *refs):
    inner_ref, outer_ref, sems = refs[-3:]
    rows = pl.ds(first, inner_ref.shape[0])

    def fetch(*raws):
        copies = [
            pltpu.make_async_copy(raw.at[rows, :], out, sems.at[i])
            for i, (raw, out) in enumerate(zip(raws, (inner_ref, outer_ref)))
        ]
        for copy in copies:
            copy.start()
        for copy in copies:
            copy.wait()

    on_even(lambda: fetch(txt_ref, img_ref), lambda: fetch(img_ref, txt_ref))


def gate_kernel(*refs):
    del refs


def first_kernel(token_ref, inner_ref, outer_ref, inner_unit, outer_unit):
    unit_rows(inner_ref, inner_unit)
    unit_rows(outer_ref, outer_unit)


def rest_kernel(*refs):
    for first_unit, rest, whole, middle, last in (refs[0::2], refs[1::2]):
        count = first_unit.shape[0]
        whole[pl.ds(0, count), :] = first_unit[...]
        unit_rows(rest, whole, count)
        middle[...] = whole[pl.ds(count, middle.shape[0]), :]
        last[...] = whole[pl.ds(count + middle.shape[0], last.shape[0]), :]


def own_kernel(temper_ref, offset_ref, img_ref, txt_ref, *outs):
    raws, sums, units, inverses, sems = outs[:2], outs[2:4], outs[4:6], outs[6:8], outs[8]
    temper, offset = temper_ref[0], offset_ref[0]

    def fetch(*sources):
        copies = [
            pltpu.make_async_copy(source, raw, sems.at[i])
            for i, (source, raw) in enumerate(zip(sources, raws))
        ]
        for copy in copies:
            copy.start()
        for copy in copies:
            copy.wait()

    on_even(lambda: fetch(txt_ref, img_ref), lambda: fetch(img_ref, txt_ref))
    for raw, unit_ref, inverse_ref in zip(raws, units, inverses):
        unit_rows(raw, unit_ref, 0, inverse_ref)

    @pl.loop(0, img_ref.shape[0] // tile)
    def _(i):
        first = pl.multiple_of(i * tile, tile)
        rows = pl.ds(first, tile)
        for side in range(2):
            others = units[1 - side][...]
            weights = weigh(units[side][rows, :], others, temper, offset, first)
            sums[side][rows, :] = jnp.dot(weights, others, preferred_element_type=jnp.float32)


def near_kernel(temper_ref, offset_ref, own_unit, sum_ref, others, out_ref):
    def finish(rows, total):
        out_ref[rows, :] = total

    attend(own_unit, others, temper_ref[0], offset_ref[0], sum_ref, finish)


def far_kernel(temper_ref, offset_ref, own_unit, sum_ref, first, middle, out_ref, others):
    def finish(rows, total):
        out_ref[rows, :] = total

    count = first.shape[0]
    others[pl.ds(0, count), :] = first[...]
    others[pl.ds(count, middle.shape[0]), :] = middle[...]
    attend(own_unit, others, temper_ref[0], offset_ref[0], sum_ref, finish)


def last_kernel(inner, temper_ref, offset_ref, own_unit, sum_ref, raw_ref, inverse_ref, *refs):
    others, *refs = refs if inner else (refs[0], *refs[3:])
    grad_img, grad_txt, ready, sems = refs
    temper = temper_ref[0]

    def run(into):
        copies = []

        def finish(rows, total):
            raw = raw_ref[rows, :].astype(jnp.float32)
            inverse = inverse_ref[rows, :]
            scale = temper * inverse
            groups = [slice(low, low + lanes) for low in range(0, raw.shape[1], lanes)]
            along = jnp.sum(
                sum(raw[:, group] * total[:, group] for group in groups), axis=1, keepdims=True
            )
            back = scale * inverse * inverse * along
            for group in groups:
                ready[rows, group] = scale * total[:, group] - back * raw[:, group]
            copies.append(
                pltpu.make_async_copy(ready.at[rows, :], into.at[rows, :], sems.at[len(copies)])
            )
            copies[-1].start()

        attend(own_unit, others, temper, offset_ref[0], sum_ref, finish, last_tiles)
        for copy in copies:
            copy.wait()

    into_txt, into_img = functools.partial(run, grad_txt), functools.partial(run, grad_img)
    on_even(into_txt, into_img) if inner else on_even(into_img, into_txt)


scalar = pl.BlockSpec(memory_space=pltpu.SMEM)
on_chip = pl.BlockSpec(memory_space=pltpu.VMEM)
off_chip = pl.BlockSpec(memory_space=pltpu.HBM)
anywhere = pl.BlockSpec(memory_space=pl.ANY)


def pinned(*values, memory=pltpu.VMEM):
    return [pltpu.with_memory_space_constraint(value, memory) for value in values]


def limit(mebibytes):
    return pltpu.CompilerParams(vmem_limit_bytes=mebibytes * 2**20)


def costs(rows, others, width, weight):
    return pl.CostEstimate(
        flops=int(weight * rows * others * width),
        bytes_accessed=4 * rows * width,
        transcendentals=0,
    )


small = pl.CostEstimate(flops=0, bytes_accessed=2**10, transcendentals=0)


def held(rows, like, dtype=jnp.bfloat16):
    return pltpu.VMEM((rows, like.shape[1]), dtype)


def pieces_of(images, texts, first, last, tokens):
    return pl.pallas_call(
        functools.partial(pieces_kernel, first),
        in_specs=[off_chip] * 2 + [anywhere] * len(tokens),
        out_specs=[on_chip] * 2,
        out_shape=[held(last - first, images)] * 2,
        scratch_shapes=[pltpu.SemaphoreType.DMA((2,))],
        compiler_params=limit(1),
        cost_estimate=small,
    )(*pinned(images, texts, memory=pltpu.HBM), *tokens)


def first_units(token, inner, outer):
    return pl.pallas_call(
        first_kernel,
        in_specs=[anywhere] + [on_chip] * 2,
        out_specs=[on_chip] * 2,
        out_shape=[held(inner.shape[0], inner)] * 2,
        compiler_params=limit(4),
        cost_estimate=small,
    )(token, *pinned(inner, outer))


def rest_units(firsts, rests):
    count, width = firsts[0].shape[0], firsts[0]
    more = rests[0].shape[0]
    sizes = (count + more, split - count, count + more - split)
    return pl.pallas_call(
        rest_kernel,
        in_specs=[on_chip] * 4,
        out_specs=[on_chip] * 6,
        out_shape=[held(size, width) for size in sizes for _ in range(2)],
        compiler_params=limit(4),
        cost_estimate=small,
    )(*pinned(*firsts, *rests))


def gate(token, *values):
    count = len(values)
    return pl.pallas_call(
        gate_kernel,
        in_specs=[anywhere] + [on_chip] * count,
        out_specs=[on_chip] * count,
        out_shape=[pltpu.VMEM(value.shape, value.dtype) for value in values],
        input_output_aliases={1 + i: i for i in range(count)},
        compiler_params=limit(1),
        cost_estimate=small,
    )(token, *pinned(*values))


def own_block(temper, offset, images, texts):
    rows = images.shape[0]
    raws, sums = held(rows, images), held(rows, images, jnp.float32)
    inverses = pltpu.VMEM((rows, lanes), jnp.float32)
    return pl.pallas_call(
        own_kernel,
        in_specs=[scalar] * 2 + [off_chip] * 2,
        out_specs=[on_chip] * 8,
        out_shape=[raws, raws, sums, sums, raws, raws, inverses, inverses],
        scratch_shapes=[pltpu.SemaphoreType.DMA((2,))],
        compiler_params=limit(16),
        cost_estimate=costs(rows, rows, images.shape[1], 32),
    )(temper, offset, *pinned(images, texts, memory=pltpu.HBM))


def more_block(temper, offset, unit, sums, pieces, weight):
    rows, width = unit.shape
    others = sum(piece.shape[0] for piece in pieces)
    several = len(pieces) > 1
    return pl.pallas_call(
        far_kernel if several else near_kernel,
        in_specs=[scalar] * 2 + [on_chip] * (2 + len(pieces)),
        out_specs=on_chip,
        out_shape=held(rows, unit, jnp.float32),
        input_output_aliases={3: 0},
        scratch_shapes=[pltpu.VMEM((others, width), jnp.bfloat16)] * several,
        compiler_params=limit(16),
        cost_estimate=costs(rows, others, width, weight),
    )(temper, offset, *pinned(unit, sums, *pieces))


def last_block(temper, offset, unit, sums, raw, inverse, piece, grads):
    rows, width = unit.shape
    inner = not grads
    return pl.pallas_call(
        functools.partial(last_kernel, inner),
        in_specs=[scalar] * 2 + [on_chip] * 5 + [off_chip] * len(grads),
        out_specs=[off_chip] * 2,
        out_shape=[jax.ShapeDtypeStruct((rows, width), jnp.float32)] * 2,
        input_output_aliases={} if inner else {7: 0, 8: 1},
        scratch_shapes=[
            pltpu.VMEM((rows, width), jnp.float32),
            pltpu.SemaphoreType.DMA((len(last_tiles),)),
        ],
        compiler_params=limit(16),
        cost_estimate=costs(rows, piece.shape[0], width, 16),
    )(temper, offset, *pinned(unit, sums, raw, inverse, piece), *grads)


def local(images, texts, log_scale, logit_bias):
    temper = jnp.exp(log_scale)
    rows = images.shape[0]
    pieces = pieces_of(images, texts, 0, start, [])
    pieces = [pieces[0], gate(pieces[0], pieces[1])[0]]
    firsts = [exchanged(pieces[0], True), exchanged(pieces[1], False)]
    pieces = pieces_of(images, texts, start, rows, pieces[:1])
    rests = [exchanged(pieces[0], True), exchanged(pieces[1], False)]
    raw_inner, raw_outer, sum_inner, sum_outer, unit_inner, unit_outer, inv_inner, inv_outer = (
        own_block(temper, logit_bias, images, texts)
    )
    firsts = first_units(inv_inner, *firsts)
    far_outer, far_inner = exchanged(firsts[0], False), exchanged(firsts[1], True)
    near_inner, near_outer, *middles, last_inner, last_outer = rest_units(firsts, rests)
    middle_outer, middle_inner = exchanged(middles[0], False), exchanged(middles[1], True)
    more = functools.partial(more_block, temper, logit_bias)
    sum_inner = more(unit_inner, sum_inner, [near_inner], 6)
    sum_outer = more(unit_outer, sum_outer, [near_outer], 6)
    last_inner, last_outer, far_inner, far_outer = gate(
        sum_outer, last_inner, last_outer, far_inner, far_outer
    )
    last_outer, last_inner = exchanged(last_inner, False), exchanged(last_outer, True)
    sum_inner = more(unit_inner, sum_inner, [far_inner, middle_inner], 0.01)
    (middle_outer,) = gate(sum_inner, middle_outer)
    sum_outer = more(unit_outer, sum_outer, [far_outer, middle_outer], 0.01)
    (last_inner,) = gate(sum_outer, last_inner)
    last = functools.partial(last_block, temper, logit_bias)
    grads = last(unit_inner, sum_inner, raw_inner, inv_inner, last_inner, ())
    return tuple(last(unit_outer, sum_outer, raw_outer, inv_outer, last_outer, grads))


def solution(mesh):
    return jax.shard_map(
        local,
        mesh=mesh,
        in_specs=(P(axes, None), P(axes, None), P(), P()),
        out_specs=(P(axes, None), P(axes, None)),
        check_vma=False,
    )
```
